512 devices in a mesh: seq: 16 (over z_lo, y), dp: 32 (over x, z_hi, core).
Axes of the slice: x: 4, y: 4, z: 16 (z_hi: 4, z_lo: 4; z = z_hi * 4 + z_lo), core: 2. Of those that a mesh axis runs over, the one named last changes fastest.
Arguments:
- frames: bfloat16 [32, 3072, 1536], P('dp', 'seq'), may hold values from -6 to 6
- queries: bfloat16 [32, 3072, 1536], P('dp', 'seq'), may hold values from -16 to 16
- keys: bfloat16 [32, 3072, 1536], P('dp', 'seq'), may hold values from -16 to 16
- values: bfloat16 [32, 3072, 1536], P('dp', 'seq'), may hold values from -24 to 24
- lengths: int32 [32], P('dp'), may hold values from 1536 to 3072, as said below
- out_proj: bfloat16 [1536, 1536], P(None, 'dp'), may hold values from -0.15625 to 0.15625
- conv_kernel: float32 [31, 1536], replicated, may hold values from -1 to 1
- cotangent: bfloat16 [32, 3072, 1536], P('dp', 'seq'), may hold values from -6 to 6
Outputs:
- block_out: bfloat16 [32, 3072, 1536], P('dp', 'seq')
- grad_hidden: bfloat16 [32, 3072, 1536], P('dp', 'seq')
- grad_context: bfloat16 [32, 3072, 1536], P('dp', 'seq')
- grad_kernel: float32 [31, 1536], replicated
The draws below stay inside these ranges and needn't reach their ends.
Inputs may be any that keep to these rules, and one draw needn't show every extreme that they name: `lengths`: one utterance has 3072 valid frames and another 3072 // 2.
All inputs are finite; a program needn't handle non-finite values.
Results may differ from the reference program's by a relative error of at most 0.0062.
Values may be sent and summed in bfloat16 or wider, within the bound.
No kernel may reach another device: no remote copies, remote signals or barrier semaphores. Data moves between devices by JAX's collectives and lax.ppermute only.
A program may use at most 64 MiB of HBM per device.

```python
import math
import jax
import jax.numpy as jnp
from jax import lax

D = 1536
HEADS = 16
KERNEL = 31
HEAD_DIM = 96
LENGTH = 3072
NB = 32


def drawn_pair(key):
    full_shape = (NB, LENGTH, D)
    base_query = jax.random.normal(jax.random.fold_in(key, 11), full_shape, jnp.float32)
    base_key = jax.random.normal(jax.random.fold_in(key, 12), full_shape, jnp.float32)
    return (base_query, base_key)


def draw_queries(key, part):
    return drawn_pair(key)[0].astype(jnp.bfloat16)


def draw_keys(key, part):
    return drawn_pair(key)[1].astype(jnp.bfloat16)


def draw_lengths(key, part):
    drawn = jax.random.randint(jax.random.fold_in(key, 21), (NB,), LENGTH // 2, LENGTH + 1)
    longest = jax.random.randint(jax.random.fold_in(key, 22), (), 0, NB)
    shortest = (longest + 1) % NB
    drawn = drawn.at[longest].set(LENGTH).at[shortest].set(LENGTH // 2)
    return drawn.astype(jnp.int32)


def levels(key, extent, pieces, low, high):
    level = 1.0
    for dim, shards_of in pieces:
        steps = jax.random.uniform(jax.random.fold_in(jax.random.fold_in(key, 6), dim), (shards_of,), jnp.float32, low / len(pieces), high / len(pieces))
        level = level * jnp.repeat(jnp.exp(steps), extent[dim] // shards_of).reshape((-1,) + (1,) * (len(extent) - 1 - dim))
    return level


def noise(own_key, dims, width, reach, cuts=(), kind=jnp.bfloat16):
    values = jax.random.normal(own_key, dims, jnp.float32) * width
    if len(cuts) > 0:
        values = levels(own_key, dims, cuts, -0.22, 0.18) * values
    return jnp.clip(values, min=-reach, max=reach).astype(kind)


def setup_inputs(seed: int = 0) -> dict:
    arg_keys = jax.random.split(jax.random.key(seed), 9)
    frames = noise(arg_keys[0], (NB, LENGTH, D), 1.0, 6.0, ((0, 32), (1, 16)))
    queries = draw_queries(jax.random.fold_in(arg_keys[8], 71), 0)
    keys = draw_keys(jax.random.fold_in(arg_keys[8], 71), 0)
    values = noise(arg_keys[3], (NB, LENGTH, D), 4.0, 24.0, ((0, 32), (1, 16)))
    lengths = draw_lengths(jax.random.fold_in(arg_keys[8], 71), 0)
    out_proj = noise(arg_keys[5], (D, D), D ** -0.5, 0.15625, ((1, 32),))
    conv_kernel = noise(arg_keys[6], (KERNEL, D), KERNEL ** -0.5, 1.0, (), jnp.float32)
    cotangent = noise(arg_keys[7], (NB, LENGTH, D), 1.0, 6.0, ((0, 32), (1, 16)))
    return dict(frames=frames, queries=queries, keys=keys, values=values, lengths=lengths, out_proj=out_proj, conv_kernel=conv_kernel, cotangent=cotangent)


def head_context(operands, valid_row):
    query_head, key_head, value_head = operands
    scores = jnp.dot(query_head, key_head.T, preferred_element_type=jnp.float32) * HEAD_DIM ** (-0.5)
    scores = jnp.where(valid_row[None, :], scores, -jnp.inf)
    largest = lax.optimization_barrier(jnp.max(scores, axis=-1, keepdims=True))
    expd = jnp.exp(scores - largest)
    weights = (expd / lax.optimization_barrier(jnp.sum(expd, axis=-1, keepdims=True))).astype(jnp.bfloat16)
    return jnp.dot(weights, value_head, preferred_element_type=jnp.float32).astype(jnp.bfloat16)

def split_heads(array):
    return array.reshape(LENGTH, HEADS, HEAD_DIM).transpose(1, 0, 2)

def utterance_context(operands):
    query_rows, key_rows, value_rows, valid_row = operands
    per_head = lax.map(lambda ops: head_context(ops, valid_row), (split_heads(query_rows), split_heads(key_rows), split_heads(value_rows)))
    return per_head.transpose(1, 0, 2).reshape(LENGTH, D)

def reference(frames, queries, keys, values, lengths, out_proj, conv_kernel, cotangent):
    half_width = KERNEL // 2
    positions = jnp.arange(LENGTH, dtype=jnp.int32)
    valid = positions[None, :] < lengths[:, None]
    context = lax.map(utterance_context, (queries, keys, values, valid))
    mixed = jnp.dot(context.reshape(NB * LENGTH, D), out_proj, preferred_element_type=jnp.float32).reshape(NB, LENGTH, D)
    hidden = (frames.astype(jnp.float32) + mixed).astype(jnp.bfloat16)
    conv_input = jnp.where(valid[:, :, None], hidden, jnp.zeros((), jnp.bfloat16))
    padded = jnp.pad(conv_input, ((0, 0), (half_width, half_width), (0, 0)))
    conv = jnp.zeros((NB, LENGTH, D), jnp.float32)
    for offset in range(KERNEL):
        conv = conv + conv_kernel[offset] * padded[:, offset:offset + LENGTH].astype(jnp.float32)
    sigma = jax.nn.sigmoid(conv)
    block_out = (hidden.astype(jnp.float32) + conv * sigma).astype(jnp.bfloat16)
    grad_out = cotangent.astype(jnp.float32)
    conv_grad = (grad_out * sigma * (1.0 + conv * (1.0 - sigma))).astype(jnp.bfloat16)
    grad_float = conv_grad.astype(jnp.float32)
    kernel_terms = []
    for offset in range(KERNEL):
        kernel_terms.append(lax.optimization_barrier(jnp.sum(grad_float * padded[:, offset:offset + LENGTH].astype(jnp.float32), axis=(0, 1))))
    grad_kernel = jnp.stack(kernel_terms) / math.sqrt(NB * LENGTH)
    grad_padded = jnp.pad(conv_grad, ((0, 0), (half_width, half_width), (0, 0)))
    back = jnp.zeros((NB, LENGTH, D), jnp.float32)
    for offset in range(KERNEL):
        begin = 2 * half_width - offset
        back = back + conv_kernel[offset] * grad_padded[:, begin:begin + LENGTH].astype(jnp.float32)
    grad_hidden = (grad_out + jnp.where(valid[:, :, None], back, 0.0)).astype(jnp.bfloat16)
    grad_context = jnp.dot(grad_hidden.reshape(NB * LENGTH, D), out_proj.T, preferred_element_type=jnp.float32)
    grad_context = grad_context.reshape(NB, LENGTH, D).astype(jnp.bfloat16)
    return (block_out, grad_hidden, grad_context, grad_kernel)
```

```python
import functools
import math

import jax
import jax.numpy as jnp
from jax import lax
from jax.experimental import pallas as pl
from jax.experimental.pallas import tpu as pltpu
from jax.sharding import Mesh
from jax.sharding import PartitionSpec as P

KERNEL = 31
HEAD_DIM = 96
LANES = 128
ROWS = 192
WIDTH = 1536
TILES = WIDTH // LANES
HEADS = 16
LENGTH = ROWS * HEADS
HALF = ROWS // 2
GROUP = 2 * TILES
SLAB = 144
EDGE = 32
QUERY_ROWS = 2 * ROWS
KEY_BLOCK = 512
BF16 = jnp.bfloat16
F32 = jnp.float32
SEQ = ("zl", "y")
DP = ("x", "zh", "c")


def lane_index(rows):
    return lax.broadcasted_iota(jnp.int32, (rows, LANES), 1)


def roll(block, shift):
    return pltpu.roll(block, shift, 1)


def pack_kernel(q_ref, k_ref, v_ref, out_ref):
    lane = lane_index(ROWS)
    low = lane[:SLAB] < HEAD_DIM
    for which, ref in enumerate((q_ref, k_ref, v_ref)):
        tiles = [ref[:, i * LANES : (i + 1) * LANES] for i in range(3)]
        heads = (
            tiles[0],
            roll(jnp.where(lane >= 96, tiles[0], tiles[1]), 32),
            roll(jnp.where(lane >= 64, tiles[1], tiles[2]), 64),
            roll(tiles[2], 96),
        )
        for i, head in enumerate(heads):
            rest = head[SLAB:]
            side = jnp.concatenate([roll(rest, 96), roll(rest, 64), roll(rest, 32)], axis=0)
            out_ref[i, which] = jnp.where(low, head[:SLAB], side)


def pack(queries, keys, values):
    columns = pl.BlockSpec((ROWS, 3 * LANES), lambda i: (0, i))
    return pl.pallas_call(
        pack_kernel,
        grid=(HEADS // 4,),
        in_specs=[columns] * 3,
        out_specs=pl.BlockSpec((4, 3, SLAB, LANES), lambda i: (i, 0, 0, 0)),
        out_shape=jax.ShapeDtypeStruct((HEADS, 3, SLAB, LANES), BF16),
        compiler_params=pltpu.CompilerParams(vmem_limit_bytes=60 * 2**20),
        cost_estimate=pl.CostEstimate(flops=0, bytes_accessed=100_000, transcendentals=0),
        name="pack",
    )(queries, keys, values)


def unpack(block):
    lane = lane_index(48)
    rest = jnp.where(
        lane < 32,
        roll(block[:48], 32),
        jnp.where(lane < 64, roll(block[48:96], 64), roll(block[96:], 96)),
    )
    return jnp.concatenate([block, rest], axis=0)


def attend_kernel(length_ref, qkv_ref, out_ref, kt, vs, qs, os, score_a, score_b):
    scale = math.log2(math.e) * HEAD_DIM ** (-0.5)
    lane = lane_index(ROWS)
    inside = lane < HEAD_DIM
    length = length_ref[0]
    one = jnp.where(lane == HEAD_DIM, 1.0, 0.0).astype(BF16)

    os[:EDGE] = jnp.zeros((EDGE, LANES), BF16)
    os[EDGE + LENGTH :] = jnp.zeros((EDGE, LANES), BF16)

    def prepare(source, carry):
        rows = pl.ds(pl.multiple_of(source * ROWS, 64), ROWS)
        frame = source * ROWS + lax.broadcasted_iota(jnp.int32, (ROWS, LANES), 0)
        hidden_key = jnp.where((lane == HEAD_DIM) & (frame >= length), -1e30, 0.0).astype(BF16)
        qs[rows] = jnp.where(inside, unpack(qkv_ref[source, 0]), one)
        os[pl.ds(pl.multiple_of(EDGE + source * ROWS, 32), ROWS)] = jnp.where(
            inside, unpack(qkv_ref[source, 1]), hidden_key
        )
        vs[rows] = jnp.where(inside, unpack(qkv_ref[source, 2]), one)
        return carry

    lax.fori_loop(0, HEADS, prepare, 0)
    for start in range(0, LENGTH, 256):
        kt[:, start : start + 256] = os[EDGE + start : EDGE + start + 256].T

    def score(block, ref):
        queries = qs[pl.ds(pl.multiple_of(block * QUERY_ROWS, 128), QUERY_ROWS)]
        best = jnp.full((QUERY_ROWS, LANES), -jnp.inf, F32)
        for start in range(0, LENGTH, KEY_BLOCK):
            part = jnp.dot(
                queries, kt[:, start : start + KEY_BLOCK], preferred_element_type=F32
            )
            ref[:, start : start + KEY_BLOCK] = part
            for tile in range(0, KEY_BLOCK, LANES):
                best = jnp.maximum(best, part[:, tile : tile + LANES])
        return jnp.max(best, axis=1, keepdims=True)

    def finish(block, ref, best):
        total = jnp.zeros((QUERY_ROWS, LANES), F32)
        for start in range(0, LENGTH, KEY_BLOCK):
            weights = jnp.exp2((ref[:, start : start + KEY_BLOCK] - best) * scale).astype(BF16)
            total = total + jnp.dot(
                weights, vs[start : start + KEY_BLOCK], preferred_element_type=F32
            )
        context = total / total[:, HEAD_DIM : HEAD_DIM + 1]
        os[pl.ds(pl.multiple_of(EDGE + block * QUERY_ROWS, 32), QUERY_ROWS)] = context.astype(BF16)

    blocks = LENGTH // QUERY_ROWS
    best = score(0, score_a)

    def step(i, best):
        after = score(2 * i + 1, score_b)
        finish(2 * i, score_a, best)
        best = score(2 * i + 2, score_a)
        finish(2 * i + 1, score_b, after)
        return best

    best = lax.fori_loop(0, blocks // 2 - 1, step, best)
    after = score(blocks - 1, score_b)
    finish(blocks - 2, score_a, best)
    finish(blocks - 1, score_b, after)

    halo_lane = lane_index(EDGE)

    def deliver(target, carry):
        begin = target * ROWS
        left = os[pl.ds(pl.multiple_of(begin, 32), EDGE)]
        right = os[pl.ds(pl.multiple_of(begin + EDGE + ROWS, 32), EDGE)]
        own = os[pl.ds(pl.multiple_of(begin + EDGE, 32), ROWS)]
        side = jnp.concatenate(
            [roll(part, shift) for shift in (96, 64, 32) for part in (left, right)], axis=0
        )
        out_ref[target] = jnp.where(inside, own, side)
        return carry

    lax.fori_loop(0, HEADS, deliver, 0)


def attend(length, qkv):
    return pl.pallas_call(
        attend_kernel,
        in_specs=[
            pl.BlockSpec(memory_space=pltpu.SMEM),
            pl.BlockSpec(memory_space=pltpu.VMEM),
        ],
        out_shape=jax.ShapeDtypeStruct((HEADS, ROWS, LANES), BF16),
        scratch_shapes=[
            pltpu.VMEM((LANES, LENGTH), BF16),
            pltpu.VMEM((LENGTH, LANES), BF16),
            pltpu.VMEM((LENGTH, LANES), BF16),
            pltpu.VMEM((LENGTH + 2 * EDGE, LANES), BF16),
            pltpu.VMEM((QUERY_ROWS, LENGTH), F32),
            pltpu.VMEM((QUERY_ROWS, LENGTH), F32),
        ],
        compiler_params=pltpu.CompilerParams(vmem_limit_bytes=48 * 2**20),
        cost_estimate=pl.CostEstimate(flops=0, bytes_accessed=100_000, transcendentals=0),
        name="attend",
    )(length, qkv)


X_STEPS = 160
G_STEPS = 128


def steps(ref, step, column, count=1):
    return ref[pl.ds(pl.multiple_of(step * GROUP + column * 8, 8), 8)]


def to_steps(ref, block, first, count, tile):
    for half in range(2):
        begin = first + half * HALF
        ref[pl.ds(half * TILES + tile, count, stride=GROUP)] = block[begin : begin + count]


def from_steps(ref, half, tile):
    return ref[pl.ds(half * TILES + tile, HALF, stride=GROUP)]


def forward_kernel(
    place_ref, context_ref, project_ref, frames_ref, cot_ref, taps_ref,
    plain_ref, grad_ref, terms_ref, dense, xs, hs, cs, both,
):
    first, length = place_ref[0], place_ref[1]
    rows = ROWS + 2 * EDGE
    lane = lane_index(rows)
    quarter = lane_index(2 * EDGE)
    for group in range(HEADS // 4):
        heads = []
        for i in range(4):
            block = context_ref[4 * group + i]
            halo = jnp.where(
                quarter < 32,
                roll(block[:64], 32),
                jnp.where(quarter < 64, roll(block[64:128], 64), roll(block[128:], 96)),
            )
            heads.append(jnp.concatenate([halo[:EDGE], block, halo[EDGE:]], axis=0))
        second, third, fourth = roll(heads[1], 96), roll(heads[2], 64), roll(heads[3], 32)
        base = 3 * group * LANES
        dense[:, base : base + LANES] = jnp.where(lane < 96, heads[0], second)
        dense[:, base + LANES : base + 2 * LANES] = jnp.where(lane < 64, second, third)
        dense[:, base + 2 * LANES : base + 3 * LANES] = jnp.where(lane < 32, third, fourth)

    frame = first - EDGE + lax.broadcasted_iota(jnp.int32, (rows, LANES), 0)
    valid = (frame >= 0) & (frame < length)
    across = (((1,), (1,)), ((), ()))
    wide = 512
    for start in range(0, WIDTH, wide):
        columns = slice(start, start + wide)
        mixed = lax.dot_general(
            dense[...], project_ref[columns], across, preferred_element_type=F32
        )
        hidden = (frames_ref[:, columns].astype(F32) + mixed).astype(BF16).astype(F32)
        for i in range(wide // LANES):
            tile = start // LANES + i
            block = hidden[:, i * LANES : (i + 1) * LANES]
            to_steps(xs, jnp.where(valid, block, 0.0), 0, X_STEPS, tile)
            to_steps(hs, block, 16, G_STEPS, tile)
            to_steps(
                cs, cot_ref[:, tile * LANES : (tile + 1) * LANES].astype(F32), 0, G_STEPS, tile
            )

    def convolve(index, carry):
        column = index % 3
        step = (index // 3) * 8
        window = [steps(xs, step + 1 + i, column) for i in range(8)]
        sums = [jnp.zeros((8, LANES), F32) for _ in range(8)]
        for k in range(KERNEL):
            tap = taps_ref[pl.ds(pl.multiple_of(k * GROUP + column * 8, 8), 8)]
            sums = [total + tap * value for total, value in zip(sums, window)]
            if k < KERNEL - 1:
                window = window[1:] + [steps(xs, step + k + 9, column)]
        for i, conv in enumerate(sums):
            at = pl.ds(pl.multiple_of((step + i) * GROUP + column * 8, 8), 8)
            sigma = jax.nn.sigmoid(conv)
            plain_ref[at] = hs[at] + conv * sigma
            grad = cs[at] * sigma * (1.0 + conv * (1.0 - sigma))
            grad_ref[at] = grad.astype(BF16).astype(F32)
        return carry

    lax.fori_loop(0, 3 * G_STEPS // 8, convolve, 0)

    for column in range(3):

        def gather(block, sums):
            step = block * 8
            grads = [steps(grad_ref, step + 16 + i, column) for i in range(8)]
            sums = list(sums)
            for offset in range(KERNEL + 7):
                value = steps(xs, step + 17 + offset, column)
                for i in range(8):
                    if 0 <= offset - i < KERNEL:
                        sums[offset - i] = sums[offset - i] + grads[i] * value
            return tuple(sums)

        zero = tuple(jnp.zeros((8, LANES), F32) for _ in range(KERNEL))
        sums = lax.fori_loop(0, HALF // 8, gather, zero)
        for k in range(KERNEL):
            both[k, column * 8 : column * 8 + 8] = sums[k]
    terms_ref[...] = jnp.zeros((KERNEL + 1, 16, LANES), F32)
    terms_ref[:KERNEL, :TILES] = both[:, :TILES] + both[:, TILES:]


def forward(place, context, project, frames, cotangent, taps):
    return pl.pallas_call(
        forward_kernel,
        in_specs=[pl.BlockSpec(memory_space=pltpu.SMEM)]
        + [pl.BlockSpec(memory_space=pltpu.VMEM)] * 5,
        out_shape=[
            jax.ShapeDtypeStruct((G_STEPS * GROUP, LANES), F32),
            jax.ShapeDtypeStruct((G_STEPS * GROUP, LANES), F32),
            jax.ShapeDtypeStruct((KERNEL + 1, 16, LANES), F32),
        ],
        scratch_shapes=[
            pltpu.VMEM((ROWS + 2 * EDGE, WIDTH), BF16),
            pltpu.VMEM((X_STEPS * GROUP, LANES), F32),
            pltpu.VMEM((G_STEPS * GROUP, LANES), F32),
            pltpu.VMEM((G_STEPS * GROUP, LANES), F32),
            pltpu.VMEM((KERNEL, GROUP, LANES), F32),
        ],
        compiler_params=pltpu.CompilerParams(vmem_limit_bytes=48 * 2**20),
        cost_estimate=pl.CostEstimate(
            flops=2 * 256 * WIDTH * WIDTH, bytes_accessed=10_000_000, transcendentals=400_000
        ),
        name="forward",
    )(place, context, project, frames, cotangent, taps)


def backward_kernel(
    place_ref, plain_ref, grad_ref, cot_ref, taps_ref, project_ref,
    block_ref, hidden_ref, context_ref, bs,
):
    first, length = place_ref[0], place_ref[1]

    def convolve(index, carry):
        column = index % 3
        step = (index // 3) * 8
        window = [steps(grad_ref, step + 1 + i, column) for i in range(8)]
        sums = [jnp.zeros((8, LANES), F32) for _ in range(8)]
        for k in range(KERNEL):
            tap = taps_ref[pl.ds(pl.multiple_of((KERNEL - 1 - k) * GROUP + column * 8, 8), 8)]
            sums = [total + tap * value for total, value in zip(sums, window)]
            if k < KERNEL - 1:
                window = window[1:] + [steps(grad_ref, step + k + 9, column)]
        for i, total in enumerate(sums):
            bs[pl.ds(pl.multiple_of((step + i) * GROUP + column * 8, 8), 8)] = total
        return carry

    lax.fori_loop(0, 3 * HALF // 8, convolve, 0)
    frame = first + lax.broadcasted_iota(jnp.int32, (HALF, LANES), 0)
    for half in range(2):
        rows = slice(half * HALF, (half + 1) * HALF)
        valid = frame + half * HALF < length
        for tile in range(TILES):
            columns = slice(tile * LANES, (tile + 1) * LANES)
            plain = plain_ref[pl.ds(16 * GROUP + half * TILES + tile, HALF, stride=GROUP)]
            block_ref[rows, columns] = plain.astype(BF16)
            back = jnp.where(valid, from_steps(bs, half, tile), 0.0)
            cot = cot_ref[16 + half * HALF : 16 + (half + 1) * HALF, columns].astype(F32)
            hidden_ref[rows, columns] = (cot + back).astype(BF16)
    wide = 256
    for start in range(0, WIDTH, wide):
        columns = slice(start, start + wide)
        part = jnp.dot(hidden_ref[...], project_ref[:, columns], preferred_element_type=F32)
        context_ref[:, columns] = part.astype(BF16)


def backward(place, plain, grad, cotangent, taps, project):
    return pl.pallas_call(
        backward_kernel,
        in_specs=[pl.BlockSpec(memory_space=pltpu.SMEM)]
        + [pl.BlockSpec(memory_space=pltpu.VMEM)] * 5,
        out_shape=[jax.ShapeDtypeStruct((ROWS, WIDTH), BF16)] * 3,
        scratch_shapes=[pltpu.VMEM((HALF * GROUP, LANES), F32)],
        compiler_params=pltpu.CompilerParams(vmem_limit_bytes=48 * 2**20),
        cost_estimate=pl.CostEstimate(
            flops=2 * ROWS * WIDTH * WIDTH, bytes_accessed=12_000_000, transcendentals=0
        ),
        name="backward",
    )(place, plain, grad, cotangent, taps, project)


def spread(array, axes):
    copies = jnp.broadcast_to(array[None], (lax.axis_size(axes), *array.shape))
    return lax.all_to_all(copies, axes, 0, 0, tiled=True)


def local(frames, queries, keys, values, lengths, out_proj, conv_kernel, cotangent):
    seq = lax.axis_index(SEQ)
    place = jnp.stack([seq * ROWS, lengths[0]]).astype(jnp.int32)

    project = lax.all_gather(out_proj.T, DP, axis=0, tiled=True)
    qkv = lax.all_to_all(pack(queries[0], keys[0], values[0]), SEQ, 0, 0, tiled=True)

    qkv, frames, cotangent = lax.optimization_barrier((qkv, frames, cotangent))
    edge = jnp.concatenate([frames[0, -EDGE:], cotangent[0, -16:]], axis=0)
    forward_pairs = [(i, i + 1) for i in range(HEADS - 1)]
    low = lax.ppermute(edge, SEQ, forward_pairs)
    edge = jnp.concatenate([frames[0, :EDGE], cotangent[0, :16]], axis=0)
    high = lax.ppermute(edge, SEQ, [(target, source) for source, target in forward_pairs])
    wide_frames = jnp.concatenate([low[:EDGE], frames[0], high[:EDGE]], axis=0)
    wide_cot = jnp.concatenate([low[EDGE:], cotangent[0], high[EDGE:]], axis=0)
    taps = conv_kernel.reshape(KERNEL, 1, TILES, LANES)
    taps = jnp.concatenate([taps, taps], axis=1).reshape(KERNEL * GROUP, LANES)

    heads, wide_frames, wide_cot, taps = lax.optimization_barrier(
        (attend(lengths, qkv), wide_frames, wide_cot, taps)
    )
    context = lax.all_to_all(heads, SEQ, 0, 0, tiled=True)
    plain, grad, terms = forward(place, context, project, wide_frames, wide_cot, taps)

    near_axes = ("zl", "y", "c")
    part = jnp.sum(lax.all_to_all(terms, near_axes, 0, 0, tiled=True), axis=0)
    part = jnp.sum(spread(part, ("x", "zh")), axis=0)
    block, hidden, grad_context = backward(place, plain, grad, wide_cot, taps, project)
    part, block = lax.optimization_barrier((part, block))
    whole = spread(part, near_axes)[:KERNEL, :TILES].reshape(KERNEL, WIDTH)
    grad_kernel = whole / math.sqrt(LENGTH * 32)

    return (block[None], hidden[None], grad_context[None], grad_kernel)


def solution(mesh):
    fine = Mesh(mesh.devices.reshape(4, 4, 4, 4, 2), ("zl", "y", "x", "zh", "c"))
    block = P(DP, SEQ, None)
    in_specs = (block, block, block, block, P(DP), P(None, DP), P(), block)
    out_specs = (block, block, block, P())
    return jax.shard_map(local, mesh=fine, in_specs=in_specs, out_specs=out_specs, check_vma=False)
```

```python
import functools
import math

import jax
import jax.numpy as jnp
from jax import lax
from jax.experimental import pallas as pl
from jax.experimental.pallas import tpu as pltpu
from jax.sharding import Mesh
from jax.sharding import PartitionSpec as P

KERNEL = 31
HEAD_DIM = 96
LANES = 128
ROWS = 192
WIDTH = 1536
TILES = WIDTH // LANES
HEADS = 16
LENGTH = ROWS * HEADS
HALF = ROWS // 2
GROUP = 2 * TILES
SLAB = 144
EDGE = 32
QUERY_ROWS = 2 * ROWS
KEY_BLOCK = 512
BF16 = jnp.bfloat16
F32 = jnp.float32
SEQ = ("zl", "y")
DP = ("x", "zh", "c")


def lane_index(rows):
    return lax.broadcasted_iota(jnp.int32, (rows, LANES), 1)


def roll(block, shift):
    return pltpu.roll(block, shift, 1)


def pack_kernel(q_ref, k_ref, v_ref, out_ref):
    lane = lane_index(ROWS)
    low = lane[:SLAB] < HEAD_DIM
    for which, ref in enumerate((q_ref, k_ref, v_ref)):
        tiles = [ref[:, i * LANES : (i + 1) * LANES] for i in range(3)]
        heads = (
            tiles[0],
            roll(jnp.where(lane >= 96, tiles[0], tiles[1]), 32),
            roll(jnp.where(lane >= 64, tiles[1], tiles[2]), 64),
            roll(tiles[2], 96),
        )
        for i, head in enumerate(heads):
            rest = head[SLAB:]
            side = jnp.concatenate([roll(rest, 96), roll(rest, 64), roll(rest, 32)], axis=0)
            out_ref[i, which] = jnp.where(low, head[:SLAB], side)


def pack(queries, keys, values):
    columns = pl.BlockSpec((ROWS, 3 * LANES), lambda i: (0, i))
    return pl.pallas_call(
        pack_kernel,
        grid=(HEADS // 4,),
        in_specs=[columns] * 3,
        out_specs=pl.BlockSpec((4, 3, SLAB, LANES), lambda i: (i, 0, 0, 0)),
        out_shape=jax.ShapeDtypeStruct((HEADS, 3, SLAB, LANES), BF16),
        compiler_params=pltpu.CompilerParams(vmem_limit_bytes=60 * 2**20),
        cost_estimate=pl.CostEstimate(flops=0, bytes_accessed=4_000_000, transcendentals=0),
        name="pack",
    )(queries, keys, values)


def unpack(block):
    lane = lane_index(48)
    rest = jnp.where(
        lane < 32,
        roll(block[:48], 32),
        jnp.where(lane < 64, roll(block[48:96], 64), roll(block[96:], 96)),
    )
    return jnp.concatenate([block, rest], axis=0)


def attend_kernel(length_ref, qkv_ref, out_ref, kt, vs, qs, os, score_a, score_b):
    scale = math.log2(math.e) * HEAD_DIM ** (-0.5)
    lane = lane_index(ROWS)
    inside = lane < HEAD_DIM
    length = length_ref[0]
    one = jnp.where(lane == HEAD_DIM, 1.0, 0.0).astype(BF16)

    os[:EDGE] = jnp.zeros((EDGE, LANES), BF16)
    os[EDGE + LENGTH :] = jnp.zeros((EDGE, LANES), BF16)

    def prepare(source, carry):
        rows = pl.ds(pl.multiple_of(source * ROWS, 64), ROWS)
        frame = source * ROWS + lax.broadcasted_iota(jnp.int32, (ROWS, LANES), 0)
        hidden_key = jnp.where((lane == HEAD_DIM) & (frame >= length), -1e30, 0.0).astype(BF16)
        qs[rows] = jnp.where(inside, unpack(qkv_ref[source, 0]), one)
        os[pl.ds(pl.multiple_of(EDGE + source * ROWS, 32), ROWS)] = jnp.where(
            inside, unpack(qkv_ref[source, 1]), hidden_key
        )
        vs[rows] = jnp.where(inside, unpack(qkv_ref[source, 2]), one)
        return carry

    lax.fori_loop(0, HEADS, prepare, 0)
    for start in range(0, LENGTH, 256):
        kt[:, start : start + 256] = os[EDGE + start : EDGE + start + 256].T

    def score(block, ref):
        queries = qs[pl.ds(pl.multiple_of(block * QUERY_ROWS, 128), QUERY_ROWS)]
        best = jnp.full((QUERY_ROWS, LANES), -jnp.inf, F32)
        for start in range(0, LENGTH, KEY_BLOCK):
            part = jnp.dot(
                queries, kt[:, start : start + KEY_BLOCK], preferred_element_type=F32
            )
            ref[:, start : start + KEY_BLOCK] = part
            for tile in range(0, KEY_BLOCK, LANES):
                best = jnp.maximum(best, part[:, tile : tile + LANES])
        return jnp.max(best, axis=1, keepdims=True)

    def finish(block, ref, best):
        total = jnp.zeros((QUERY_ROWS, LANES), F32)
        for start in range(0, LENGTH, KEY_BLOCK):
            weights = jnp.exp2((ref[:, start : start + KEY_BLOCK] - best) * scale).astype(BF16)
            total = total + jnp.dot(
                weights, vs[start : start + KEY_BLOCK], preferred_element_type=F32
            )
        context = total / total[:, HEAD_DIM : HEAD_DIM + 1]
        os[pl.ds(pl.multiple_of(EDGE + block * QUERY_ROWS, 32), QUERY_ROWS)] = context.astype(BF16)

    blocks = LENGTH // QUERY_ROWS
    best = score(0, score_a)

    def step(i, best):
        after = score(2 * i + 1, score_b)
        finish(2 * i, score_a, best)
        best = score(2 * i + 2, score_a)
        finish(2 * i + 1, score_b, after)
        return best

    best = lax.fori_loop(0, blocks // 2 - 1, step, best)
    after = score(blocks - 1, score_b)
    finish(blocks - 2, score_a, best)
    finish(blocks - 1, score_b, after)

    halo_lane = lane_index(EDGE)

    def deliver(target, carry):
        begin = target * ROWS
        left = os[pl.ds(pl.multiple_of(begin, 32), EDGE)]
        right = os[pl.ds(pl.multiple_of(begin + EDGE + ROWS, 32), EDGE)]
        own = os[pl.ds(pl.multiple_of(begin + EDGE, 32), ROWS)]
        side = jnp.concatenate(
            [roll(part, shift) for shift in (96, 64, 32) for part in (left, right)], axis=0
        )
        out_ref[target] = jnp.where(inside, own, side)
        return carry

    lax.fori_loop(0, HEADS, deliver, 0)


def attend(length, qkv):
    return pl.pallas_call(
        attend_kernel,
        in_specs=[
            pl.BlockSpec(memory_space=pltpu.SMEM),
            pl.BlockSpec(memory_space=pltpu.VMEM),
        ],
        out_shape=jax.ShapeDtypeStruct((HEADS, ROWS, LANES), BF16),
        scratch_shapes=[
            pltpu.VMEM((LANES, LENGTH), BF16),
            pltpu.VMEM((LENGTH, LANES), BF16),
            pltpu.VMEM((LENGTH, LANES), BF16),
            pltpu.VMEM((LENGTH + 2 * EDGE, LANES), BF16),
            pltpu.VMEM((QUERY_ROWS, LENGTH), F32),
            pltpu.VMEM((QUERY_ROWS, LENGTH), F32),
        ],
        compiler_params=pltpu.CompilerParams(vmem_limit_bytes=48 * 2**20),
        cost_estimate=pl.CostEstimate(
            flops=4 * LENGTH * LENGTH * 128,
            bytes_accessed=3_000_000,
            transcendentals=LENGTH * LENGTH,
        ),
        name="attend",
    )(length, qkv)


BLOCK = WIDTH // 4

X_STEPS = 160
G_STEPS = 128


def steps(ref, step, column, count=1):
    return ref[pl.ds(pl.multiple_of(step * GROUP + column * 8, 8), 8)]


def to_steps(ref, block, first, count, tile):
    for half in range(2):
        begin = first + half * HALF
        ref[pl.ds(half * TILES + tile, count, stride=GROUP)] = block[begin : begin + count]


def project_blocks(x, refs):
    blocks = []
    for shift, (near, far) in enumerate(zip(refs[:4], refs[4:])):
        start = pl.multiple_of(lax.rem(x + 4 - shift, 4) * BLOCK, LANES)
        blocks.append((start, BLOCK, near, far))
    return blocks


def from_steps(ref, half, tile):
    return ref[pl.ds(half * TILES + tile, HALF, stride=GROUP)]


def forward_kernel(place_ref, context_ref, frames_ref, cot_ref, taps_ref, *refs):
    project_refs, (plain_ref, grad_ref, terms_ref, dense, xs, hs, cs, both) = refs[:8], refs[8:]
    x, core, first, length = place_ref[0], place_ref[1], place_ref[2], place_ref[3]
    rows = ROWS + 2 * EDGE
    lane = lane_index(rows)
    quarter = lane_index(2 * EDGE)
    for group in range(HEADS // 4):
        heads = []
        for i in range(4):
            block = context_ref[4 * group + i]
            halo = jnp.where(
                quarter < 32,
                roll(block[:64], 32),
                jnp.where(quarter < 64, roll(block[64:128], 64), roll(block[128:], 96)),
            )
            heads.append(jnp.concatenate([halo[:EDGE], block, halo[EDGE:]], axis=0))
        second, third, fourth = roll(heads[1], 96), roll(heads[2], 64), roll(heads[3], 32)
        base = 3 * group * LANES
        dense[:, base : base + LANES] = jnp.where(lane < 96, heads[0], second)
        dense[:, base + LANES : base + 2 * LANES] = jnp.where(lane < 64, second, third)
        dense[:, base + 2 * LANES : base + 3 * LANES] = jnp.where(lane < 32, third, fourth)

    frame = first - EDGE + lax.broadcasted_iota(jnp.int32, (rows, LANES), 0)
    valid = (frame >= 0) & (frame < length)
    for tile in range(TILES):
        block = cot_ref[:, tile * LANES : (tile + 1) * LANES].astype(F32)
        to_steps(cs, block, 0, G_STEPS, tile)
    across = (((1,), (1,)), ((), ()))
    half_width = WIDTH // 2
    near = dense[:, pl.ds(pl.multiple_of(core * half_width, LANES), half_width)]
    far = dense[:, pl.ds(pl.multiple_of((1 - core) * half_width, LANES), half_width)]
    for start, wide, near_ref, far_ref in project_blocks(x, project_refs):
        mixed = lax.dot_general(near, near_ref[...], across, preferred_element_type=F32)
        mixed += lax.dot_general(far, far_ref[...], across, preferred_element_type=F32)
        columns = frames_ref[:, pl.ds(start, wide)]
        hidden = (columns.astype(F32) + mixed).astype(BF16).astype(F32)
        for i in range(wide // LANES):
            tile = start // LANES + i
            block = hidden[:, i * LANES : (i + 1) * LANES]
            to_steps(xs, jnp.where(valid, block, 0.0), 0, X_STEPS, tile)
            to_steps(hs, block, 16, G_STEPS, tile)

    def convolve(index, carry):
        column = index % 3
        step = (index // 3) * 8
        window = [steps(xs, step + 1 + i, column) for i in range(8)]
        sums = [jnp.zeros((8, LANES), F32) for _ in range(8)]
        for k in range(KERNEL):
            tap = taps_ref[pl.ds(pl.multiple_of(k * GROUP + column * 8, 8), 8)]
            sums = [total + tap * value for total, value in zip(sums, window)]
            if k < KERNEL - 1:
                window = window[1:] + [steps(xs, step + k + 9, column)]
        for i, conv in enumerate(sums):
            at = pl.ds(pl.multiple_of((step + i) * GROUP + column * 8, 8), 8)
            sigma = jax.nn.sigmoid(conv)
            plain_ref[at] = hs[at] + conv * sigma
            grad = cs[at] * sigma * (1.0 + conv * (1.0 - sigma))
            grad_ref[at] = grad.astype(BF16).astype(F32)
        return carry

    lax.fori_loop(0, 3 * G_STEPS // 8, convolve, 0)

    for column in range(3):

        def gather(block, sums):
            step = block * 8
            grads = [steps(grad_ref, step + 16 + i, column) for i in range(8)]
            sums = list(sums)
            for offset in range(KERNEL + 7):
                value = steps(xs, step + 17 + offset, column)
                for i in range(8):
                    if 0 <= offset - i < KERNEL:
                        sums[offset - i] = sums[offset - i] + grads[i] * value
            return tuple(sums)

        zero = tuple(jnp.zeros((8, LANES), F32) for _ in range(KERNEL))
        sums = lax.fori_loop(0, HALF // 8, gather, zero)
        for k in range(KERNEL):
            both[k, column * 8 : column * 8 + 8] = sums[k]
    terms_ref[...] = jnp.zeros((KERNEL + 1, 16, LANES), F32)
    terms_ref[:KERNEL, :TILES] = both[:, :TILES] + both[:, TILES:]


def forward(place, context, frames, cotangent, taps, project):
    return pl.pallas_call(
        forward_kernel,
        in_specs=[pl.BlockSpec(memory_space=pltpu.SMEM)]
        + [pl.BlockSpec(memory_space=pltpu.VMEM)] * 12,
        out_shape=[
            jax.ShapeDtypeStruct((G_STEPS * GROUP, LANES), F32),
            jax.ShapeDtypeStruct((G_STEPS * GROUP, LANES), F32),
            jax.ShapeDtypeStruct((KERNEL + 1, 16, LANES), F32),
        ],
        scratch_shapes=[
            pltpu.VMEM((ROWS + 2 * EDGE, WIDTH), BF16),
            pltpu.VMEM((X_STEPS * GROUP, LANES), F32),
            pltpu.VMEM((G_STEPS * GROUP, LANES), F32),
            pltpu.VMEM((G_STEPS * GROUP, LANES), F32),
            pltpu.VMEM((KERNEL, GROUP, LANES), F32),
        ],
        compiler_params=pltpu.CompilerParams(vmem_limit_bytes=48 * 2**20),
        cost_estimate=pl.CostEstimate(
            flops=2 * 256 * WIDTH * WIDTH, bytes_accessed=10_000_000, transcendentals=400_000
        ),
        name="forward",
    )(place, context, frames, cotangent, taps, *project)


def backward_kernel(place_ref, plain_ref, grad_ref, cot_ref, taps_ref, *refs):
    project_refs, (block_ref, hidden_ref, context_ref, bs) = refs[:8], refs[8:]
    x, core, first, length = place_ref[0], place_ref[1], place_ref[2], place_ref[3]

    def convolve(index, carry):
        column = index % 3
        step = (index // 3) * 8
        window = [steps(grad_ref, step + 1 + i, column) for i in range(8)]
        sums = [jnp.zeros((8, LANES), F32) for _ in range(8)]
        for k in range(KERNEL):
            tap = taps_ref[pl.ds(pl.multiple_of((KERNEL - 1 - k) * GROUP + column * 8, 8), 8)]
            sums = [total + tap * value for total, value in zip(sums, window)]
            if k < KERNEL - 1:
                window = window[1:] + [steps(grad_ref, step + k + 9, column)]
        for i, total in enumerate(sums):
            bs[pl.ds(pl.multiple_of((step + i) * GROUP + column * 8, 8), 8)] = total
        return carry

    lax.fori_loop(0, 3 * HALF // 8, convolve, 0)
    frame = first + lax.broadcasted_iota(jnp.int32, (HALF, LANES), 0)
    for half in range(2):
        rows = slice(half * HALF, (half + 1) * HALF)
        valid = frame + half * HALF < length
        for tile in range(TILES):
            columns = slice(tile * LANES, (tile + 1) * LANES)
            plain = plain_ref[pl.ds(16 * GROUP + half * TILES + tile, HALF, stride=GROUP)]
            block_ref[rows, columns] = plain.astype(BF16)
            back = jnp.where(valid, from_steps(bs, half, tile), 0.0)
            cot = cot_ref[16 + half * HALF : 16 + (half + 1) * HALF, columns].astype(F32)
            hidden_ref[rows, columns] = (cot + back).astype(BF16)
    half_width = WIDTH // 2
    blocks = [
        (hidden_ref[:, pl.ds(start, wide)], near_ref, far_ref)
        for start, wide, near_ref, far_ref in project_blocks(x, project_refs)
    ]
    step = 256
    for which, begin in ((1, core * half_width), (2, (1 - core) * half_width)):
        for start in range(0, half_width, step):
            total = jnp.zeros((ROWS, step), F32)
            for block in blocks:
                part = block[which][:, start : start + step]
                total = total + jnp.dot(block[0], part, preferred_element_type=F32)
            columns = pl.ds(pl.multiple_of(begin + start, LANES), step)
            context_ref[:, columns] = total.astype(BF16)


def backward(place, plain, grad, cotangent, taps, project):
    return pl.pallas_call(
        backward_kernel,
        in_specs=[pl.BlockSpec(memory_space=pltpu.SMEM)]
        + [pl.BlockSpec(memory_space=pltpu.VMEM)] * 12,
        out_shape=[jax.ShapeDtypeStruct((ROWS, WIDTH), BF16)] * 3,
        scratch_shapes=[pltpu.VMEM((HALF * GROUP, LANES), F32)],
        compiler_params=pltpu.CompilerParams(vmem_limit_bytes=48 * 2**20),
        cost_estimate=pl.CostEstimate(
            flops=2 * ROWS * WIDTH * WIDTH, bytes_accessed=12_000_000, transcendentals=0
        ),
        name="backward",
    )(place, plain, grad, cotangent, taps, *project)


def spread(array, axes):
    copies = jnp.broadcast_to(array[None], (lax.axis_size(axes), *array.shape))
    return lax.all_to_all(copies, axes, 0, 0, tiled=True)


def local(frames, queries, keys, values, lengths, out_proj, conv_kernel, cotangent):
    seq = lax.axis_index(SEQ)
    core = lax.axis_index("c")
    place = jnp.stack([lax.axis_index("x"), core, seq * ROWS, lengths[0]]).astype(jnp.int32)

    rows = lax.all_gather(out_proj.T, "c", axis=0, tiled=True)
    quarter = rows.shape[0] // 4
    share = lax.dynamic_slice(
        rows, (lax.axis_index("y") * quarter, core * (WIDTH // 2)), (quarter, WIDTH // 2)
    )
    queries, keys, values, share = lax.optimization_barrier((queries, keys, values, share))
    zh = lax.axis_index("zh")
    other = lax.ppermute(share, "zh", [(0, 1), (1, 0), (2, 3), (3, 2)])
    pair = jnp.where(zh % 2 == 0, jnp.stack([share, other]), jnp.stack([other, share]))
    rest = lax.ppermute(pair, "zh", [(1, 2), (2, 1), (3, 0), (0, 3)])
    packed, rest = lax.optimization_barrier((pack(queries[0], keys[0], values[0]), rest))
    qkv = lax.all_to_all(packed, SEQ, 0, 0, tiled=True)
    share = jnp.where(zh < 2, jnp.concatenate([pair, rest]), jnp.concatenate([rest, pair]))
    share = lax.all_gather(share, "y")
    share = share.transpose(1, 0, 2, 3).reshape(BLOCK, WIDTH // 2)
    near = [share]
    for shift in (1, 2, 3):
        near.append(lax.ppermute(share, "x", [(i, (i + shift) % 4) for i in range(4)]))

    edge = jnp.concatenate([frames[0, -EDGE:], cotangent[0, -16:]], axis=0)
    forward_pairs = [(i, i + 1) for i in range(HEADS - 1)]
    low = lax.ppermute(edge, SEQ, forward_pairs)
    edge = jnp.concatenate([frames[0, :EDGE], cotangent[0, :16]], axis=0)
    high = lax.ppermute(edge, SEQ, [(target, source) for source, target in forward_pairs])
    wide_frames = jnp.concatenate([low[:EDGE], frames[0], high[:EDGE]], axis=0)
    wide_cot = jnp.concatenate([low[EDGE:], cotangent[0], high[EDGE:]], axis=0)
    taps = conv_kernel.reshape(KERNEL, 1, TILES, LANES)
    taps = jnp.concatenate([taps, taps], axis=1).reshape(KERNEL * GROUP, LANES)

    swap = [(0, 1), (1, 0)]
    far = [lax.ppermute(share, "c", swap)]
    qkv, far, wide_frames, wide_cot, taps = lax.optimization_barrier(
        (qkv, far, wide_frames, wide_cot, taps)
    )
    heads, near = lax.optimization_barrier((attend(lengths, qkv), near))
    project = near + far + [lax.ppermute(block, "c", swap) for block in near[1:]]

    context = lax.all_to_all(heads, SEQ, 0, 0, tiled=True)
    plain, grad, terms = forward(place, context, wide_frames, wide_cot, taps, project)

    near_axes = ("zl", "y", "c")
    part = jnp.sum(lax.all_to_all(terms, near_axes, 0, 0, tiled=True), axis=0)
    part = jnp.sum(spread(part, ("x", "zh")), axis=0)
    block, hidden, grad_context = backward(place, plain, grad, wide_cot, taps, project)
    part, block = lax.optimization_barrier((part, block))
    whole = spread(part, near_axes)[:KERNEL, :TILES].reshape(KERNEL, WIDTH)
    grad_kernel = whole / math.sqrt(LENGTH * 32)

    return (block[None], hidden[None], grad_context[None], grad_kernel)


def solution(mesh):
    fine = Mesh(mesh.devices.reshape(4, 4, 4, 4, 2), ("zl", "y", "x", "zh", "c"))
    block = P(DP, SEQ, None)
    in_specs = (block, block, block, block, P(DP), P(None, DP), P(), block)
    out_specs = (block, block, block, P())
    return jax.shard_map(local, mesh=fine, in_specs=in_specs, out_specs=out_specs, check_vma=False)
```

```python
import functools
import math

import jax
import jax.numpy as jnp
from jax import lax
from jax.experimental import pallas as pl
from jax.experimental.pallas import tpu as pltpu
from jax.sharding import Mesh
from jax.sharding import PartitionSpec as P

KERNEL = 31
HEAD_DIM = 96
LANES = 128
ROWS = 192
WIDTH = 1536
TILES = WIDTH // LANES
HEADS = 16
LENGTH = ROWS * HEADS
HALF = ROWS // 2
GROUP = 2 * TILES
SLAB = 144
EDGE = 32
QUERY_ROWS = 4 * ROWS
KEY_BLOCK = 512
BF16 = jnp.bfloat16
F32 = jnp.float32
SEQ = ("zl", "y")
DP = ("x", "zh", "c")


def lane_index(rows):
    return lax.broadcasted_iota(jnp.int32, (rows, LANES), 1)


def roll(block, shift):
    return pltpu.roll(block, shift, 1)


def pack_kernel(q_ref, k_ref, v_ref, out_ref):
    lane = lane_index(ROWS)
    low = lane[:SLAB] < HEAD_DIM
    for which, ref in enumerate((q_ref, k_ref, v_ref)):
        tiles = [ref[:, i * LANES : (i + 1) * LANES] for i in range(3)]
        heads = (
            tiles[0],
            roll(jnp.where(lane >= 96, tiles[0], tiles[1]), 32),
            roll(jnp.where(lane >= 64, tiles[1], tiles[2]), 64),
            roll(tiles[2], 96),
        )
        for i, head in enumerate(heads):
            rest = head[SLAB:]
            side = jnp.concatenate([roll(rest, 96), roll(rest, 64), roll(rest, 32)], axis=0)
            out_ref[i, which] = jnp.where(low, head[:SLAB], side)


def pack(queries, keys, values):
    columns = pl.BlockSpec((ROWS, 3 * LANES), lambda i: (0, i))
    return pl.pallas_call(
        pack_kernel,
        grid=(HEADS // 4,),
        in_specs=[columns] * 3,
        out_specs=pl.BlockSpec((4, 3, SLAB, LANES), lambda i: (i, 0, 0, 0)),
        out_shape=jax.ShapeDtypeStruct((HEADS, 3, SLAB, LANES), BF16),
        compiler_params=pltpu.CompilerParams(vmem_limit_bytes=60 * 2**20),
        cost_estimate=pl.CostEstimate(flops=0, bytes_accessed=4_000_000, transcendentals=0),
        name="pack",
    )(queries, keys, values)


def unpack(block):
    lane = lane_index(48)
    rest = jnp.where(
        lane < 32,
        roll(block[:48], 32),
        jnp.where(lane < 64, roll(block[48:96], 64), roll(block[96:], 96)),
    )
    return jnp.concatenate([block, rest], axis=0)


def attend_kernel(length_ref, qkv_ref, out_ref, kt, vs, qs, os, score_a, score_b):
    scale = math.log2(math.e) * HEAD_DIM ** (-0.5)
    lane = lane_index(ROWS)
    inside = lane < HEAD_DIM
    length = length_ref[0]
    one = jnp.where(lane == HEAD_DIM, 1.0, 0.0).astype(BF16)

    os[:EDGE] = jnp.zeros((EDGE, LANES), BF16)
    os[EDGE + LENGTH :] = jnp.zeros((EDGE, LANES), BF16)

    def prepare(source, carry):
        rows = pl.ds(pl.multiple_of(source * ROWS, 64), ROWS)
        frame = source * ROWS + lax.broadcasted_iota(jnp.int32, (ROWS, LANES), 0)
        hidden_key = jnp.where((lane == HEAD_DIM) & (frame >= length), -1e30, 0.0).astype(BF16)
        qs[rows] = jnp.where(inside, unpack(qkv_ref[source, 0]), one)
        os[pl.ds(pl.multiple_of(EDGE + source * ROWS, 32), ROWS)] = jnp.where(
            inside, unpack(qkv_ref[source, 1]), hidden_key
        )
        vs[rows] = jnp.where(inside, unpack(qkv_ref[source, 2]), one)
        return carry

    lax.fori_loop(0, HEADS, prepare, 0)
    for start in range(0, LENGTH, 256):
        kt[:, start : start + 256] = os[EDGE + start : EDGE + start + 256].T

    def score(block, ref):
        queries = qs[pl.ds(pl.multiple_of(block * QUERY_ROWS, 128), QUERY_ROWS)]
        best = jnp.full((QUERY_ROWS, LANES), -jnp.inf, F32)
        for start in range(0, LENGTH, KEY_BLOCK):
            part = jnp.dot(
                queries, kt[:, start : start + KEY_BLOCK], preferred_element_type=F32
            )
            ref[:, start : start + KEY_BLOCK] = part
            for tile in range(0, KEY_BLOCK, LANES):
                best = jnp.maximum(best, part[:, tile : tile + LANES])
        return jnp.max(best, axis=1, keepdims=True)

    def finish(block, ref, best):
        total = jnp.zeros((QUERY_ROWS, LANES), F32)
        for start in range(0, LENGTH, KEY_BLOCK):
            weights = jnp.exp2((ref[:, start : start + KEY_BLOCK] - best) * scale).astype(BF16)
            total = total + jnp.dot(
                weights, vs[start : start + KEY_BLOCK], preferred_element_type=F32
            )
        context = total / total[:, HEAD_DIM : HEAD_DIM + 1]
        os[pl.ds(pl.multiple_of(EDGE + block * QUERY_ROWS, 32), QUERY_ROWS)] = context.astype(BF16)

    blocks = LENGTH // QUERY_ROWS
    best = score(0, score_a)

    def step(i, best):
        after = score(2 * i + 1, score_b)
        finish(2 * i, score_a, best)
        best = score(2 * i + 2, score_a)
        finish(2 * i + 1, score_b, after)
        return best

    best = lax.fori_loop(0, blocks // 2 - 1, step, best)
    after = score(blocks - 1, score_b)
    finish(blocks - 2, score_a, best)
    finish(blocks - 1, score_b, after)

    halo_lane = lane_index(EDGE)

    def deliver(target, carry):
        begin = target * ROWS
        left = os[pl.ds(pl.multiple_of(begin, 32), EDGE)]
        right = os[pl.ds(pl.multiple_of(begin + EDGE + ROWS, 32), EDGE)]
        own = os[pl.ds(pl.multiple_of(begin + EDGE, 32), ROWS)]
        side = jnp.concatenate(
            [roll(part, shift) for shift in (96, 64, 32) for part in (left, right)], axis=0
        )
        out_ref[target] = jnp.where(inside, own, side)
        return carry

    lax.fori_loop(0, HEADS, deliver, 0)


def attend(length, qkv):
    return pl.pallas_call(
        attend_kernel,
        in_specs=[
            pl.BlockSpec(memory_space=pltpu.SMEM),
            pl.BlockSpec(memory_space=pltpu.VMEM),
        ],
        out_shape=jax.ShapeDtypeStruct((HEADS, ROWS, LANES), BF16),
        scratch_shapes=[
            pltpu.VMEM((LANES, LENGTH), BF16),
            pltpu.VMEM((LENGTH, LANES), BF16),
            pltpu.VMEM((LENGTH, LANES), BF16),
            pltpu.VMEM((LENGTH + 2 * EDGE, LANES), BF16),
            pltpu.VMEM((QUERY_ROWS, LENGTH), F32),
            pltpu.VMEM((QUERY_ROWS, LENGTH), F32),
        ],
        compiler_params=pltpu.CompilerParams(vmem_limit_bytes=48 * 2**20),
        cost_estimate=pl.CostEstimate(
            flops=4 * LENGTH * LENGTH * 128,
            bytes_accessed=3_000_000,
            transcendentals=LENGTH * LENGTH,
        ),
        name="attend",
    )(length, qkv)


BLOCK = WIDTH // 4

X_STEPS = 160
G_STEPS = 128


def steps(ref, step, column, count=1):
    return ref[pl.ds(pl.multiple_of(step * GROUP + column * 8, 8), 8)]


def to_steps(ref, block, first, count, tile):
    for half in range(2):
        begin = first + half * HALF
        ref[pl.ds(half * TILES + tile, count, stride=GROUP)] = block[begin : begin + count]


def project_blocks(x, refs):
    blocks = []
    for shift, (near, far) in enumerate(zip(refs[:4], refs[4:])):
        start = pl.multiple_of(lax.rem(x + 4 - shift, 4) * BLOCK, LANES)
        blocks.append((start, BLOCK, near, far))
    return blocks


def from_steps(ref, half, tile):
    return ref[pl.ds(half * TILES + tile, HALF, stride=GROUP)]


def forward_kernel(place_ref, context_ref, frames_ref, cot_ref, taps_ref, *refs):
    project_refs, (plain_ref, grad_ref, terms_ref, dense, xs, hs, cs, both) = refs[:8], refs[8:]
    x, core, first, length = place_ref[0], place_ref[1], place_ref[2], place_ref[3]
    rows = ROWS + 2 * EDGE
    lane = lane_index(rows)
    quarter = lane_index(2 * EDGE)
    for group in range(HEADS // 4):
        heads = []
        for i in range(4):
            block = context_ref[4 * group + i]
            halo = jnp.where(
                quarter < 32,
                roll(block[:64], 32),
                jnp.where(quarter < 64, roll(block[64:128], 64), roll(block[128:], 96)),
            )
            heads.append(jnp.concatenate([halo[:EDGE], block, halo[EDGE:]], axis=0))
        second, third, fourth = roll(heads[1], 96), roll(heads[2], 64), roll(heads[3], 32)
        base = 3 * group * LANES
        dense[:, base : base + LANES] = jnp.where(lane < 96, heads[0], second)
        dense[:, base + LANES : base + 2 * LANES] = jnp.where(lane < 64, second, third)
        dense[:, base + 2 * LANES : base + 3 * LANES] = jnp.where(lane < 32, third, fourth)

    frame = first - EDGE + lax.broadcasted_iota(jnp.int32, (rows, LANES), 0)
    valid = (frame >= 0) & (frame < length)
    for tile in range(TILES):
        block = cot_ref[:, tile * LANES : (tile + 1) * LANES].astype(F32)
        to_steps(cs, block, 0, G_STEPS, tile)
    across = (((1,), (1,)), ((), ()))
    half_width = WIDTH // 2
    near = dense[:, pl.ds(pl.multiple_of(core * half_width, LANES), half_width)]
    far = dense[:, pl.ds(pl.multiple_of((1 - core) * half_width, LANES), half_width)]
    for start, wide, near_ref, far_ref in project_blocks(x, project_refs):
        mixed = lax.dot_general(near, near_ref[...], across, preferred_element_type=F32)
        mixed += lax.dot_general(far, far_ref[...], across, preferred_element_type=F32)
        columns = frames_ref[:, pl.ds(start, wide)]
        hidden = (columns.astype(F32) + mixed).astype(BF16).astype(F32)
        for i in range(wide // LANES):
            tile = start // LANES + i
            block = hidden[:, i * LANES : (i + 1) * LANES]
            to_steps(xs, jnp.where(valid, block, 0.0), 0, X_STEPS, tile)
            to_steps(hs, block, 16, G_STEPS, tile)

    def convolve(index, carry):
        column = index % 3
        step = (index // 3) * 8
        window = [steps(xs, step + 1 + i, column) for i in range(8)]
        sums = [jnp.zeros((8, LANES), F32) for _ in range(8)]
        for k in range(KERNEL):
            tap = taps_ref[pl.ds(pl.multiple_of(k * GROUP + column * 8, 8), 8)]
            sums = [total + tap * value for total, value in zip(sums, window)]
            if k < KERNEL - 1:
                window = window[1:] + [steps(xs, step + k + 9, column)]
        for i, conv in enumerate(sums):
            at = pl.ds(pl.multiple_of((step + i) * GROUP + column * 8, 8), 8)
            sigma = jax.nn.sigmoid(conv)
            plain_ref[at] = hs[at] + conv * sigma
            grad = cs[at] * sigma * (1.0 + conv * (1.0 - sigma))
            grad_ref[at] = grad.astype(BF16).astype(F32)
        return carry

    lax.fori_loop(0, 3 * G_STEPS // 8, convolve, 0)

    for column in range(3):

        def gather(block, sums):
            step = block * 8
            grads = [steps(grad_ref, step + 16 + i, column) for i in range(8)]
            sums = list(sums)
            for offset in range(KERNEL + 7):
                value = steps(xs, step + 17 + offset, column)
                for i in range(8):
                    if 0 <= offset - i < KERNEL:
                        sums[offset - i] = sums[offset - i] + grads[i] * value
            return tuple(sums)

        zero = tuple(jnp.zeros((8, LANES), F32) for _ in range(KERNEL))
        sums = lax.fori_loop(0, HALF // 8, gather, zero)
        for k in range(KERNEL):
            both[k, column * 8 : column * 8 + 8] = sums[k]
    terms_ref[...] = jnp.zeros((KERNEL + 1, 16, LANES), F32)
    terms_ref[:KERNEL, :TILES] = both[:, :TILES] + both[:, TILES:]


def forward(place, context, frames, cotangent, taps, project):
    return pl.pallas_call(
        forward_kernel,
        in_specs=[pl.BlockSpec(memory_space=pltpu.SMEM)]
        + [pl.BlockSpec(memory_space=pltpu.VMEM)] * 12,
        out_shape=[
            jax.ShapeDtypeStruct((G_STEPS * GROUP, LANES), F32),
            jax.ShapeDtypeStruct((G_STEPS * GROUP, LANES), F32),
            jax.ShapeDtypeStruct((KERNEL + 1, 16, LANES), F32),
        ],
        scratch_shapes=[
            pltpu.VMEM((ROWS + 2 * EDGE, WIDTH), BF16),
            pltpu.VMEM((X_STEPS * GROUP, LANES), F32),
            pltpu.VMEM((G_STEPS * GROUP, LANES), F32),
            pltpu.VMEM((G_STEPS * GROUP, LANES), F32),
            pltpu.VMEM((KERNEL, GROUP, LANES), F32),
        ],
        compiler_params=pltpu.CompilerParams(vmem_limit_bytes=48 * 2**20),
        cost_estimate=pl.CostEstimate(
            flops=2 * 256 * WIDTH * WIDTH, bytes_accessed=10_000_000, transcendentals=400_000
        ),
        name="forward",
    )(place, context, frames, cotangent, taps, *project)


def backward_kernel(place_ref, plain_ref, grad_ref, cot_ref, taps_ref, *refs):
    project_refs, (block_ref, hidden_ref, context_ref, bs) = refs[:8], refs[8:]
    x, core, first, length = place_ref[0], place_ref[1], place_ref[2], place_ref[3]

    def convolve(index, carry):
        column = index % 3
        step = (index // 3) * 8
        window = [steps(grad_ref, step + 1 + i, column) for i in range(8)]
        sums = [jnp.zeros((8, LANES), F32) for _ in range(8)]
        for k in range(KERNEL):
            tap = taps_ref[pl.ds(pl.multiple_of((KERNEL - 1 - k) * GROUP + column * 8, 8), 8)]
            sums = [total + tap * value for total, value in zip(sums, window)]
            if k < KERNEL - 1:
                window = window[1:] + [steps(grad_ref, step + k + 9, column)]
        for i, total in enumerate(sums):
            bs[pl.ds(pl.multiple_of((step + i) * GROUP + column * 8, 8), 8)] = total
        return carry

    lax.fori_loop(0, 3 * HALF // 8, convolve, 0)
    frame = first + lax.broadcasted_iota(jnp.int32, (HALF, LANES), 0)
    for half in range(2):
        rows = slice(half * HALF, (half + 1) * HALF)
        valid = frame + half * HALF < length
        for tile in range(TILES):
            columns = slice(tile * LANES, (tile + 1) * LANES)
            plain = plain_ref[pl.ds(16 * GROUP + half * TILES + tile, HALF, stride=GROUP)]
            block_ref[rows, columns] = plain.astype(BF16)
            back = jnp.where(valid, from_steps(bs, half, tile), 0.0)
            cot = cot_ref[16 + half * HALF : 16 + (half + 1) * HALF, columns].astype(F32)
            hidden_ref[rows, columns] = (cot + back).astype(BF16)
    half_width = WIDTH // 2
    blocks = [
        (hidden_ref[:, pl.ds(start, wide)], near_ref, far_ref)
        for start, wide, near_ref, far_ref in project_blocks(x, project_refs)
    ]
    step = 256
    for which, begin in ((1, core * half_width), (2, (1 - core) * half_width)):
        for start in range(0, half_width, step):
            total = jnp.zeros((ROWS, step), F32)
            for block in blocks:
                part = block[which][:, start : start + step]
                total = total + jnp.dot(block[0], part, preferred_element_type=F32)
            columns = pl.ds(pl.multiple_of(begin + start, LANES), step)
            context_ref[:, columns] = total.astype(BF16)


def backward(place, plain, grad, cotangent, taps, project):
    return pl.pallas_call(
        backward_kernel,
        in_specs=[pl.BlockSpec(memory_space=pltpu.SMEM)]
        + [pl.BlockSpec(memory_space=pltpu.VMEM)] * 12,
        out_shape=[jax.ShapeDtypeStruct((ROWS, WIDTH), BF16)] * 3,
        scratch_shapes=[pltpu.VMEM((HALF * GROUP, LANES), F32)],
        compiler_params=pltpu.CompilerParams(vmem_limit_bytes=48 * 2**20),
        cost_estimate=pl.CostEstimate(
            flops=2 * ROWS * WIDTH * WIDTH, bytes_accessed=12_000_000, transcendentals=0
        ),
        name="backward",
    )(place, plain, grad, cotangent, taps, *project)


def spread(array, axes):
    copies = jnp.broadcast_to(array[None], (lax.axis_size(axes), *array.shape))
    return lax.all_to_all(copies, axes, 0, 0, tiled=True)


def local(frames, queries, keys, values, lengths, out_proj, conv_kernel, cotangent):
    seq = lax.axis_index(SEQ)
    core = lax.axis_index("c")
    place = jnp.stack([lax.axis_index("x"), core, seq * ROWS, lengths[0]]).astype(jnp.int32)

    rows = lax.all_gather(out_proj.T, "c", axis=0, tiled=True)
    quarter = rows.shape[0] // 4
    share = lax.dynamic_slice(
        rows, (lax.axis_index("y") * quarter, core * (WIDTH // 2)), (quarter, WIDTH // 2)
    )
    queries, keys, values, share = lax.optimization_barrier((queries, keys, values, share))
    zh = lax.axis_index("zh")
    other = lax.ppermute(share, "zh", [(0, 1), (1, 0), (2, 3), (3, 2)])
    pair = jnp.where(zh % 2 == 0, jnp.stack([share, other]), jnp.stack([other, share]))
    rest = lax.ppermute(pair, "zh", [(1, 2), (2, 1), (3, 0), (0, 3)])
    packed, rest = lax.optimization_barrier((pack(queries[0], keys[0], values[0]), rest))
    qkv = lax.all_to_all(packed, SEQ, 0, 0, tiled=True)
    share = jnp.where(zh < 2, jnp.concatenate([pair, rest]), jnp.concatenate([rest, pair]))
    share = lax.all_gather(share, "y")
    share = share.transpose(1, 0, 2, 3).reshape(BLOCK, WIDTH // 2)
    near = [share]
    for shift in (1, 2, 3):
        near.append(lax.ppermute(share, "x", [(i, (i + shift) % 4) for i in range(4)]))

    taps = conv_kernel.reshape(KERNEL, 1, TILES, LANES)
    taps = jnp.concatenate([taps, taps], axis=1).reshape(KERNEL * GROUP, LANES)

    swap = [(0, 1), (1, 0)]
    far = [lax.ppermute(share, "c", swap)]
    qkv, far, taps = lax.optimization_barrier((qkv, far, taps))
    heads, near, frames, cotangent = lax.optimization_barrier(
        (attend(lengths, qkv), near, frames, cotangent)
    )
    project = near + far + [lax.ppermute(block, "c", swap) for block in near[1:]]

    edge = jnp.concatenate([frames[0, -EDGE:], cotangent[0, -16:]], axis=0)
    forward_pairs = [(i, i + 1) for i in range(HEADS - 1)]
    low = lax.ppermute(edge, SEQ, forward_pairs)
    edge = jnp.concatenate([frames[0, :EDGE], cotangent[0, :16]], axis=0)
    high = lax.ppermute(edge, SEQ, [(target, source) for source, target in forward_pairs])
    wide_frames = jnp.concatenate([low[:EDGE], frames[0], high[:EDGE]], axis=0)
    wide_cot = jnp.concatenate([low[EDGE:], cotangent[0], high[EDGE:]], axis=0)

    context = lax.all_to_all(heads, SEQ, 0, 0, tiled=True)
    plain, grad, terms = forward(place, context, wide_frames, wide_cot, taps, project)

    near_axes = ("zl", "y", "c")
    part = jnp.sum(lax.all_to_all(terms, near_axes, 0, 0, tiled=True), axis=0)
    part = jnp.sum(spread(part, ("x", "zh")), axis=0)
    block, hidden, grad_context = backward(place, plain, grad, wide_cot, taps, project)
    part, block = lax.optimization_barrier((part, block))
    whole = spread(part, near_axes)[:KERNEL, :TILES].reshape(KERNEL, WIDTH)
    grad_kernel = whole / math.sqrt(LENGTH * 32)

    return (block[None], hidden[None], grad_context[None], grad_kernel)


def solution(mesh):
    fine = Mesh(mesh.devices.reshape(4, 4, 4, 4, 2), ("zl", "y", "x", "zh", "c"))
    block = P(DP, SEQ, None)
    in_specs = (block, block, block, block, P(DP), P(None, DP), P(), block)
    out_specs = (block, block, block, P())
    return jax.shard_map(local, mesh=fine, in_specs=in_specs, out_specs=out_specs, check_vma=False)
```

```python
import functools
import math

import jax
import jax.numpy as jnp
from jax import lax
from jax.experimental import pallas as pl
from jax.experimental.pallas import tpu as pltpu
from jax.sharding import Mesh
from jax.sharding import PartitionSpec as P

KERNEL = 31
HEAD_DIM = 96
LANES = 128
ROWS = 192
WIDTH = 1536
TILES = WIDTH // LANES
HEADS = 16
LENGTH = ROWS * HEADS
HALF = ROWS // 2
GROUP = 2 * TILES
SLAB = 144
EDGE = 32
QUERY_ROWS = 4 * ROWS
KEY_BLOCK = 512
BF16 = jnp.bfloat16
F32 = jnp.float32
SEQ = ("zl", "y")
DP = ("x", "zh", "c")


def lane_index(rows):
    return lax.broadcasted_iota(jnp.int32, (rows, LANES), 1)


def roll(block, shift):
    return pltpu.roll(block, shift, 1)


def pack_kernel(q_ref, k_ref, v_ref, out_ref):
    lane = lane_index(ROWS)
    low = lane[:SLAB] < HEAD_DIM
    for which, ref in enumerate((q_ref, k_ref, v_ref)):
        tiles = [ref[:, i * LANES : (i + 1) * LANES] for i in range(3)]
        heads = (
            tiles[0],
            roll(jnp.where(lane >= 96, tiles[0], tiles[1]), 32),
            roll(jnp.where(lane >= 64, tiles[1], tiles[2]), 64),
            roll(tiles[2], 96),
        )
        for i, head in enumerate(heads):
            rest = head[SLAB:]
            side = jnp.concatenate([roll(rest, 96), roll(rest, 64), roll(rest, 32)], axis=0)
            out_ref[i, which] = jnp.where(low, head[:SLAB], side)


def pack(queries, keys, values):
    columns = pl.BlockSpec((ROWS, 3 * LANES), lambda i: (0, i))
    return pl.pallas_call(
        pack_kernel,
        grid=(HEADS // 4,),
        in_specs=[columns] * 3,
        out_specs=pl.BlockSpec((4, 3, SLAB, LANES), lambda i: (i, 0, 0, 0)),
        out_shape=jax.ShapeDtypeStruct((HEADS, 3, SLAB, LANES), BF16),
        compiler_params=pltpu.CompilerParams(vmem_limit_bytes=60 * 2**20),
        cost_estimate=pl.CostEstimate(flops=0, bytes_accessed=4_000_000, transcendentals=0),
        name="pack",
    )(queries, keys, values)


def unpack(block):
    lane = lane_index(48)
    rest = jnp.where(
        lane < 32,
        roll(block[:48], 32),
        jnp.where(lane < 64, roll(block[48:96], 64), roll(block[96:], 96)),
    )
    return jnp.concatenate([block, rest], axis=0)


def attend_kernel(length_ref, qkv_ref, out_ref, kt, vs, qs, os, score_a, score_b):
    scale = math.log2(math.e) * HEAD_DIM ** (-0.5)
    lane = lane_index(ROWS)
    inside = lane < HEAD_DIM
    length = length_ref[0]
    one = jnp.where(lane == HEAD_DIM, 1.0, 0.0).astype(BF16)

    os[:EDGE] = jnp.zeros((EDGE, LANES), BF16)
    os[EDGE + LENGTH :] = jnp.zeros((EDGE, LANES), BF16)

    def prepare(source, carry):
        rows = pl.ds(pl.multiple_of(source * ROWS, 64), ROWS)
        frame = source * ROWS + lax.broadcasted_iota(jnp.int32, (ROWS, LANES), 0)
        hidden_key = jnp.where((lane == HEAD_DIM) & (frame >= length), -1e30, 0.0).astype(BF16)
        qs[rows] = jnp.where(inside, unpack(qkv_ref[source, 0]), one)
        os[pl.ds(pl.multiple_of(EDGE + source * ROWS, 32), ROWS)] = jnp.where(
            inside, unpack(qkv_ref[source, 1]), hidden_key
        )
        vs[rows] = jnp.where(inside, unpack(qkv_ref[source, 2]), one)
        return carry

    lax.fori_loop(0, HEADS, prepare, 0)
    for start in range(0, LENGTH, 256):
        kt[:, start : start + 256] = os[EDGE + start : EDGE + start + 256].T

    def score(block, ref):
        queries = qs[pl.ds(pl.multiple_of(block * QUERY_ROWS, 128), QUERY_ROWS)]
        best = jnp.full((QUERY_ROWS, LANES), -jnp.inf, F32)
        for start in range(0, LENGTH, KEY_BLOCK):
            part = jnp.dot(
                queries, kt[:, start : start + KEY_BLOCK], preferred_element_type=F32
            )
            ref[:, start : start + KEY_BLOCK] = part
            for tile in range(0, KEY_BLOCK, LANES):
                best = jnp.maximum(best, part[:, tile : tile + LANES])
        return jnp.max(best, axis=1, keepdims=True)

    def finish(block, ref, best):
        total = jnp.zeros((QUERY_ROWS, LANES), F32)
        for start in range(0, LENGTH, KEY_BLOCK):
            weights = jnp.exp2((ref[:, start : start + KEY_BLOCK] - best) * scale).astype(BF16)
            total = total + jnp.dot(
                weights, vs[start : start + KEY_BLOCK], preferred_element_type=F32
            )
        context = total / total[:, HEAD_DIM : HEAD_DIM + 1]
        os[pl.ds(pl.multiple_of(EDGE + block * QUERY_ROWS, 32), QUERY_ROWS)] = context.astype(BF16)

    blocks = LENGTH // QUERY_ROWS
    best = score(0, score_a)

    def step(i, best):
        after = score(2 * i + 1, score_b)
        finish(2 * i, score_a, best)
        best = score(2 * i + 2, score_a)
        finish(2 * i + 1, score_b, after)
        return best

    best = lax.fori_loop(0, blocks // 2 - 1, step, best)
    after = score(blocks - 1, score_b)
    finish(blocks - 2, score_a, best)
    finish(blocks - 1, score_b, after)

    halo_lane = lane_index(EDGE)

    def deliver(target, carry):
        begin = target * ROWS
        left = os[pl.ds(pl.multiple_of(begin, 32), EDGE)]
        right = os[pl.ds(pl.multiple_of(begin + EDGE + ROWS, 32), EDGE)]
        own = os[pl.ds(pl.multiple_of(begin + EDGE, 32), ROWS)]
        side = jnp.concatenate(
            [roll(part, shift) for shift in (96, 64, 32) for part in (left, right)], axis=0
        )
        out_ref[target] = jnp.where(inside, own, side)
        return carry

    lax.fori_loop(0, HEADS, deliver, 0)


def attend(length, qkv):
    return pl.pallas_call(
        attend_kernel,
        in_specs=[
            pl.BlockSpec(memory_space=pltpu.SMEM),
            pl.BlockSpec(memory_space=pltpu.VMEM),
        ],
        out_shape=jax.ShapeDtypeStruct((HEADS, ROWS, LANES), BF16),
        scratch_shapes=[
            pltpu.VMEM((LANES, LENGTH), BF16),
            pltpu.VMEM((LENGTH, LANES), BF16),
            pltpu.VMEM((LENGTH, LANES), BF16),
            pltpu.VMEM((LENGTH + 2 * EDGE, LANES), BF16),
            pltpu.VMEM((QUERY_ROWS, LENGTH), F32),
            pltpu.VMEM((QUERY_ROWS, LENGTH), F32),
        ],
        compiler_params=pltpu.CompilerParams(vmem_limit_bytes=48 * 2**20),
        cost_estimate=pl.CostEstimate(
            flops=4 * LENGTH * LENGTH * 128,
            bytes_accessed=3_000_000,
            transcendentals=LENGTH * LENGTH,
        ),
        name="attend",
    )(length, qkv)


BLOCK = WIDTH // 4

X_STEPS = 160
G_STEPS = 128


def steps(ref, step, column, count=1):
    return ref[pl.ds(pl.multiple_of(step * GROUP + column * 8, 8), 8)]


def to_steps(ref, block, first, count, tile):
    for half in range(2):
        begin = first + half * HALF
        ref[pl.ds(half * TILES + tile, count, stride=GROUP)] = block[begin : begin + count]


def project_blocks(x, refs):
    blocks = []
    for shift, (near, far) in enumerate(zip(refs[:4], refs[4:])):
        start = pl.multiple_of(lax.rem(x + 4 - shift, 4) * BLOCK, LANES)
        blocks.append((start, BLOCK, near, far))
    return blocks


def from_steps(ref, half, tile):
    return ref[pl.ds(half * TILES + tile, HALF, stride=GROUP)]


def forward_kernel(
    place_ref, context_ref, low_ref, high_ref, frames_ref, cot_ref, taps_ref, *refs
):
    project_refs, (plain_ref, grad_ref, terms_ref, dense, xs, hs, cs, both) = refs[:8], refs[8:]
    x, core, first, length = place_ref[0], place_ref[1], place_ref[2], place_ref[3]
    rows = ROWS + 2 * EDGE
    lane = lane_index(rows)
    quarter = lane_index(2 * EDGE)
    for group in range(HEADS // 4):
        heads = []
        for i in range(4):
            block = context_ref[4 * group + i]
            halo = jnp.where(
                quarter < 32,
                roll(block[:64], 32),
                jnp.where(quarter < 64, roll(block[64:128], 64), roll(block[128:], 96)),
            )
            heads.append(jnp.concatenate([halo[:EDGE], block, halo[EDGE:]], axis=0))
        second, third, fourth = roll(heads[1], 96), roll(heads[2], 64), roll(heads[3], 32)
        base = 3 * group * LANES
        dense[:, base : base + LANES] = jnp.where(lane < 96, heads[0], second)
        dense[:, base + LANES : base + 2 * LANES] = jnp.where(lane < 64, second, third)
        dense[:, base + 2 * LANES : base + 3 * LANES] = jnp.where(lane < 32, third, fourth)

    frame = first - EDGE + lax.broadcasted_iota(jnp.int32, (rows, LANES), 0)
    valid = (frame >= 0) & (frame < length)
    for tile in range(TILES):
        columns = slice(tile * LANES, (tile + 1) * LANES)
        block = jnp.concatenate(
            [low_ref[EDGE:, columns], cot_ref[:, columns], high_ref[EDGE:, columns]], axis=0
        )
        to_steps(cs, block.astype(F32), 0, G_STEPS, tile)
    across = (((1,), (1,)), ((), ()))
    half_width = WIDTH // 2
    near = dense[:, pl.ds(pl.multiple_of(core * half_width, LANES), half_width)]
    far = dense[:, pl.ds(pl.multiple_of((1 - core) * half_width, LANES), half_width)]
    for start, wide, near_ref, far_ref in project_blocks(x, project_refs):
        mixed = lax.dot_general(near, near_ref[...], across, preferred_element_type=F32)
        mixed += lax.dot_general(far, far_ref[...], across, preferred_element_type=F32)
        columns = pl.ds(start, wide)
        stream = jnp.concatenate(
            [low_ref[:EDGE, columns], frames_ref[:, columns], high_ref[:EDGE, columns]], axis=0
        )
        hidden = (stream.astype(F32) + mixed).astype(BF16).astype(F32)
        for i in range(wide // LANES):
            tile = start // LANES + i
            block = hidden[:, i * LANES : (i + 1) * LANES]
            to_steps(xs, jnp.where(valid, block, 0.0), 0, X_STEPS, tile)
            to_steps(hs, block, 16, G_STEPS, tile)

    def convolve(index, carry):
        column = index % 3
        step = (index // 3) * 8
        window = [steps(xs, step + 1 + i, column) for i in range(8)]
        sums = [jnp.zeros((8, LANES), F32) for _ in range(8)]
        for k in range(KERNEL):
            tap = taps_ref[pl.ds(pl.multiple_of(k * GROUP + column * 8, 8), 8)]
            sums = [total + tap * value for total, value in zip(sums, window)]
            if k < KERNEL - 1:
                window = window[1:] + [steps(xs, step + k + 9, column)]
        for i, conv in enumerate(sums):
            at = pl.ds(pl.multiple_of((step + i) * GROUP + column * 8, 8), 8)
            sigma = jax.nn.sigmoid(conv)
            plain_ref[at] = hs[at] + conv * sigma
            grad = cs[at] * sigma * (1.0 + conv * (1.0 - sigma))
            grad_ref[at] = grad.astype(BF16).astype(F32)
        return carry

    lax.fori_loop(0, 3 * G_STEPS // 8, convolve, 0)

    for column in range(3):

        def gather(block, sums):
            step = block * 8
            grads = [steps(grad_ref, step + 16 + i, column) for i in range(8)]
            sums = list(sums)
            for offset in range(KERNEL + 7):
                value = steps(xs, step + 17 + offset, column)
                for i in range(8):
                    if 0 <= offset - i < KERNEL:
                        sums[offset - i] = sums[offset - i] + grads[i] * value
            return tuple(sums)

        zero = tuple(jnp.zeros((8, LANES), F32) for _ in range(KERNEL))
        sums = lax.fori_loop(0, HALF // 8, gather, zero)
        for k in range(KERNEL):
            both[k, column * 8 : column * 8 + 8] = sums[k]
    terms_ref[...] = jnp.zeros((KERNEL + 1, 16, LANES), F32)
    terms_ref[:KERNEL, :TILES] = both[:, :TILES] + both[:, TILES:]


def forward(place, context, low, high, frames, cotangent, taps, project):
    return pl.pallas_call(
        forward_kernel,
        in_specs=[pl.BlockSpec(memory_space=pltpu.SMEM)]
        + [pl.BlockSpec(memory_space=pltpu.VMEM)] * 14,
        out_shape=[
            jax.ShapeDtypeStruct((G_STEPS * GROUP, LANES), F32),
            jax.ShapeDtypeStruct((G_STEPS * GROUP, LANES), F32),
            jax.ShapeDtypeStruct((KERNEL + 1, 16, LANES), F32),
        ],
        scratch_shapes=[
            pltpu.VMEM((ROWS + 2 * EDGE, WIDTH), BF16),
            pltpu.VMEM((X_STEPS * GROUP, LANES), F32),
            pltpu.VMEM((G_STEPS * GROUP, LANES), F32),
            pltpu.VMEM((G_STEPS * GROUP, LANES), F32),
            pltpu.VMEM((KERNEL, GROUP, LANES), F32),
        ],
        compiler_params=pltpu.CompilerParams(vmem_limit_bytes=48 * 2**20),
        cost_estimate=pl.CostEstimate(
            flops=2 * 256 * WIDTH * WIDTH, bytes_accessed=10_000_000, transcendentals=400_000
        ),
        name="forward",
    )(place, context, low, high, frames, cotangent, taps, *project)


def backward_kernel(place_ref, plain_ref, grad_ref, cot_ref, taps_ref, *refs):
    project_refs, (block_ref, hidden_ref, context_ref, bs) = refs[:8], refs[8:]
    x, core, first, length = place_ref[0], place_ref[1], place_ref[2], place_ref[3]

    def convolve(index, carry):
        column = index % 3
        step = (index // 3) * 8
        window = [steps(grad_ref, step + 1 + i, column) for i in range(8)]
        sums = [jnp.zeros((8, LANES), F32) for _ in range(8)]
        for k in range(KERNEL):
            tap = taps_ref[pl.ds(pl.multiple_of((KERNEL - 1 - k) * GROUP + column * 8, 8), 8)]
            sums = [total + tap * value for total, value in zip(sums, window)]
            if k < KERNEL - 1:
                window = window[1:] + [steps(grad_ref, step + k + 9, column)]
        for i, total in enumerate(sums):
            bs[pl.ds(pl.multiple_of((step + i) * GROUP + column * 8, 8), 8)] = total
        return carry

    lax.fori_loop(0, 3 * HALF // 8, convolve, 0)
    frame = first + lax.broadcasted_iota(jnp.int32, (HALF, LANES), 0)
    for half in range(2):
        rows = slice(half * HALF, (half + 1) * HALF)
        valid = frame + half * HALF < length
        for tile in range(TILES):
            columns = slice(tile * LANES, (tile + 1) * LANES)
            plain = plain_ref[pl.ds(16 * GROUP + half * TILES + tile, HALF, stride=GROUP)]
            block_ref[rows, columns] = plain.astype(BF16)
            back = jnp.where(valid, from_steps(bs, half, tile), 0.0)
            cot = cot_ref[rows, columns].astype(F32)
            hidden_ref[rows, columns] = (cot + back).astype(BF16)
    half_width = WIDTH // 2
    blocks = [
        (hidden_ref[:, pl.ds(start, wide)], near_ref, far_ref)
        for start, wide, near_ref, far_ref in project_blocks(x, project_refs)
    ]
    step = 256
    for which, begin in ((1, core * half_width), (2, (1 - core) * half_width)):
        for start in range(0, half_width, step):
            total = jnp.zeros((ROWS, step), F32)
            for block in blocks:
                part = block[which][:, start : start + step]
                total = total + jnp.dot(block[0], part, preferred_element_type=F32)
            columns = pl.ds(pl.multiple_of(begin + start, LANES), step)
            context_ref[:, columns] = total.astype(BF16)


def backward(place, plain, grad, cotangent, taps, project):
    return pl.pallas_call(
        backward_kernel,
        in_specs=[pl.BlockSpec(memory_space=pltpu.SMEM)]
        + [pl.BlockSpec(memory_space=pltpu.VMEM)] * 12,
        out_shape=[jax.ShapeDtypeStruct((ROWS, WIDTH), BF16)] * 3,
        scratch_shapes=[pltpu.VMEM((HALF * GROUP, LANES), F32)],
        compiler_params=pltpu.CompilerParams(vmem_limit_bytes=48 * 2**20),
        cost_estimate=pl.CostEstimate(
            flops=2 * ROWS * WIDTH * WIDTH, bytes_accessed=12_000_000, transcendentals=0
        ),
        name="backward",
    )(place, plain, grad, cotangent, taps, *project)


def spread(array, axes):
    copies = jnp.broadcast_to(array[None], (lax.axis_size(axes), *array.shape))
    return lax.all_to_all(copies, axes, 0, 0, tiled=True)


def local(frames, queries, keys, values, lengths, out_proj, conv_kernel, cotangent):
    seq = lax.axis_index(SEQ)
    core = lax.axis_index("c")
    place = jnp.stack([lax.axis_index("x"), core, seq * ROWS, lengths[0]]).astype(jnp.int32)

    rows = lax.all_gather(out_proj.T, "c", axis=0, tiled=True)
    quarter = rows.shape[0] // 4
    share = lax.dynamic_slice(
        rows, (lax.axis_index("y") * quarter, core * (WIDTH // 2)), (quarter, WIDTH // 2)
    )
    queries, keys, values, share = lax.optimization_barrier((queries, keys, values, share))
    zh = lax.axis_index("zh")
    other = lax.ppermute(share, "zh", [(0, 1), (1, 0), (2, 3), (3, 2)])
    pair = jnp.where(zh % 2 == 0, jnp.stack([share, other]), jnp.stack([other, share]))
    rest = lax.ppermute(pair, "zh", [(1, 2), (2, 1), (3, 0), (0, 3)])
    packed, rest = lax.optimization_barrier((pack(queries[0], keys[0], values[0]), rest))
    qkv = lax.all_to_all(packed, SEQ, 0, 0, tiled=True)
    share = jnp.where(zh < 2, jnp.concatenate([pair, rest]), jnp.concatenate([rest, pair]))
    share = lax.all_gather(share, "y")
    share = share.transpose(1, 0, 2, 3).reshape(BLOCK, WIDTH // 2)
    near = [share]
    for shift in (1, 2, 3):
        near.append(lax.ppermute(share, "x", [(i, (i + shift) % 4) for i in range(4)]))

    taps = conv_kernel.reshape(KERNEL, 1, TILES, LANES)
    taps = jnp.concatenate([taps, taps], axis=1).reshape(KERNEL * GROUP, LANES)

    swap = [(0, 1), (1, 0)]
    far = [lax.ppermute(share, "c", swap)]
    qkv, far, taps = lax.optimization_barrier((qkv, far, taps))
    heads, near, frames, cotangent = lax.optimization_barrier(
        (attend(lengths, qkv), near, frames, cotangent)
    )
    project = near + far + [lax.ppermute(block, "c", swap) for block in near[1:]]

    edge = jnp.concatenate([frames[0, -EDGE:], cotangent[0, -16:]], axis=0)
    forward_pairs = [(i, i + 1) for i in range(HEADS - 1)]
    low = lax.ppermute(edge, SEQ, forward_pairs)
    edge = jnp.concatenate([frames[0, :EDGE], cotangent[0, :16]], axis=0)
    high = lax.ppermute(edge, SEQ, [(target, source) for source, target in forward_pairs])

    context = lax.all_to_all(heads, SEQ, 0, 0, tiled=True)
    plain, grad, terms = forward(
        place, context, low, high, frames[0], cotangent[0], taps, project
    )

    near_axes = ("zl", "y", "c")
    part = jnp.sum(lax.all_to_all(terms, near_axes, 0, 0, tiled=True), axis=0)
    part = jnp.sum(spread(part, ("x", "zh")), axis=0)
    block, hidden, grad_context = backward(place, plain, grad, cotangent[0], taps, project)
    part, block = lax.optimization_barrier((part, block))
    whole = spread(part, near_axes)[:KERNEL, :TILES].reshape(KERNEL, WIDTH)
    grad_kernel = whole / math.sqrt(LENGTH * 32)

    return (block[None], hidden[None], grad_context[None], grad_kernel)


def solution(mesh):
    fine = Mesh(mesh.devices.reshape(4, 4, 4, 4, 2), ("zl", "y", "x", "zh", "c"))
    block = P(DP, SEQ, None)
    in_specs = (block, block, block, block, P(DP), P(None, DP), P(), block)
    out_specs = (block, block, block, P())
    return jax.shard_map(local, mesh=fine, in_specs=in_specs, out_specs=out_specs, check_vma=False)
```
